128 devices in a mesh: frame: 8 (over x_lo, z), row: 16 (over y, x_hi, core).
Axes of the slice: x: 4 (x_hi: 2, x_lo: 2; x = x_hi * 2 + x_lo), y: 4, z: 4, core: 2. Of those that a mesh axis runs over, the one named last changes fastest.
Arguments:
- tokens_a: bfloat16 [32, 2048, 1152], P('frame', 'row'), may hold values from -6 to 6
- modulate_a: float32 [3, 1152], replicated, may hold values from -3 to 3
- spatial_qkv: bfloat16 [1152, 3456], replicated, may hold values from -0.1875 to 0.1875
- spatial_proj: bfloat16 [1152, 1152], replicated, may hold values from -0.1875 to 0.1875
- spatial_gain: float32 [2, 72], replicated, may hold values from 1 to 10
- tokens_b: bfloat16 [32, 2048, 1152], P('frame', 'row'), may hold values from -6 to 6
- modulation_rows_b: float32 [3, 1152], replicated, may hold values from -3 to 3
- temporal_qkv: bfloat16 [1152, 3456], replicated, may hold values from -0.1875 to 0.1875
- temporal_proj: bfloat16 [1152, 1152], replicated, may hold values from -0.1875 to 0.1875
- temporal_gain: float32 [2, 72], replicated, may hold values from 1 to 10
Outputs:
- result_a: bfloat16 [32, 2048, 1152], P('frame', 'row')
- result_b: bfloat16 [32, 2048, 1152], P('frame', 'row')
The draws below stay inside these ranges and needn't reach their ends.
All inputs are finite; a program needn't handle non-finite values.
Results may differ from the reference program's by a relative error of at most 0.012.
The reference program's roundings to bfloat16 on the way count: a program that leaves them out, or rounds other values in their place, can miss the bound.
Values may be sent and summed in bfloat16 or wider, within the bound.
A program may use at most 128 MiB of HBM per device.

```python
import jax
import jax.numpy as jnp
from jax import lax

D = 1152
HEADS = 16
FRAMES = 32
SPOTS = 2048


def gain_table(key, upper):
    unit = jax.random.uniform(key, (2, D // HEADS), jnp.float32)
    return jnp.exp(unit * jnp.log(jnp.float32(upper)))


def draw_spatial_gain(key, part):
    key = jax.random.fold_in(key, 11)
    return gain_table(key, 3.0)


def draw_temporal_gain(key, part):
    key = jax.random.fold_in(key, 23)
    return gain_table(key, 3.0)


def levels(own_key, dims, shards, least, top_value):
    level = 1.0
    for dim, shards_of in shards:
        heights = jax.random.uniform(jax.random.fold_in(jax.random.fold_in(own_key, 6), dim), (shards_of,), jnp.float32, least / len(shards), top_value / len(shards))
        level = level * jnp.repeat(jnp.exp(heights), dims[dim] // shards_of).reshape((-1,) + (1,) * (len(dims) - 1 - dim))
    return level


def gaussian(stream_key, dims, scale, reach, cuts=(), dtype=jnp.bfloat16):
    values = jax.random.normal(stream_key, dims, jnp.float32) * scale
    if len(cuts) > 0:
        values = levels(stream_key, dims, cuts, -0.22, 0.18) * values
    return jnp.clip(values, min=-reach, max=reach).astype(dtype)


def setup_inputs(seed: int = 0) -> dict:
    arg_keys = jax.random.split(jax.random.key(seed), 11)
    tokens_a = gaussian(arg_keys[0], (FRAMES, SPOTS, D), 1.0, 6.0, ((0, 8), (1, 16)))
    modulate_a = gaussian(arg_keys[1], (3, D), 0.5, 3.0, (), jnp.float32)
    spatial_qkv = gaussian(arg_keys[2], (D, 3 * D), D ** -0.5, 0.1875)
    spatial_proj = gaussian(arg_keys[3], (D, D), D ** -0.5, 0.1875)
    spatial_gain = draw_spatial_gain(jax.random.fold_in(arg_keys[10], 71), 0)
    tokens_b = gaussian(arg_keys[5], (FRAMES, SPOTS, D), 1.0, 6.0, ((0, 8), (1, 16)))
    modulation_rows_b = gaussian(arg_keys[6], (3, D), 0.5, 3.0, (), jnp.float32)
    temporal_qkv = gaussian(arg_keys[7], (D, 3 * D), D ** -0.5, 0.1875)
    temporal_proj = gaussian(arg_keys[8], (D, D), D ** -0.5, 0.1875)
    temporal_gain = draw_temporal_gain(jax.random.fold_in(arg_keys[10], 71), 0)
    return dict(tokens_a=tokens_a, modulate_a=modulate_a, spatial_qkv=spatial_qkv, spatial_proj=spatial_proj, spatial_gain=spatial_gain, tokens_b=tokens_b, modulation_rows_b=modulation_rows_b, temporal_qkv=temporal_qkv, temporal_proj=temporal_proj, temporal_gain=temporal_gain)


def modulate(tokens, shift_scale):
    value_rows = tokens.astype(jnp.float32)
    center = value_rows - lax.optimization_barrier(jnp.mean(value_rows, axis=-1, keepdims=True))
    spread = lax.optimization_barrier(jnp.mean(center * center, axis=-1, keepdims=True))
    normed = center * lax.rsqrt(spread + 1e-06)
    return (normed * (1.0 + shift_scale[1]) + shift_scale[0]).astype(jnp.bfloat16)

def qk_normalize(projected, gains):
    lead = projected.shape[:-2]
    parts = projected.reshape(lead + (3, HEADS, D // HEADS))
    query_rows = parts[..., 0, :, :]
    key_rows = parts[..., 1, :, :]
    value_rows = parts[..., 2, :, :]
    query_rows = query_rows * lax.rsqrt(lax.optimization_barrier(jnp.mean(query_rows * query_rows, axis=-1, keepdims=True)) + 1e-06) * gains[0]
    key_rows = key_rows * lax.rsqrt(lax.optimization_barrier(jnp.mean(key_rows * key_rows, axis=-1, keepdims=True)) + 1e-06) * gains[1]
    stacked = jnp.stack([query_rows, key_rows, value_rows], axis=-3)
    return stacked.reshape(lead + (3, D)).astype(jnp.bfloat16)

def attend_rows(query_rows, key_rows, value_rows):
    logit_scores = jnp.dot(query_rows, key_rows.T, preferred_element_type=jnp.float32) / jnp.sqrt(jnp.float32(D // HEADS))
    top = lax.optimization_barrier(jnp.max(logit_scores, axis=-1, keepdims=True))
    weights = jnp.exp(logit_scores - top)
    attention_probabilities = (weights / lax.optimization_barrier(jnp.sum(weights, axis=-1, keepdims=True))).astype(jnp.bfloat16)
    return jnp.dot(attention_probabilities, value_rows, preferred_element_type=jnp.float32).astype(jnp.bfloat16)

def attend_long(query_rows, key_rows, value_rows):
    length = query_rows.shape[0]
    block = 512 if length % 512 == 0 else length
    pieces = query_rows.reshape(length // block, block, query_rows.shape[1])
    outs = lax.map(lambda piece: attend_rows(piece, key_rows, value_rows), pieces)
    return outs.reshape(length, query_rows.shape[1])

def attend_frames(query_rows, key_rows, value_rows):
    logit_scores = jnp.einsum('nsz,njz->nsj', query_rows.astype(jnp.float32), key_rows.astype(jnp.float32))
    logit_scores = logit_scores / jnp.sqrt(jnp.float32(D // HEADS))
    top = lax.optimization_barrier(jnp.max(logit_scores, axis=-1, keepdims=True))
    weights = jnp.exp(logit_scores - top)
    attention_probabilities = (weights / lax.optimization_barrier(jnp.sum(weights, axis=-1, keepdims=True))).astype(jnp.bfloat16)
    return jnp.einsum('ruv,rvs->rus', attention_probabilities.astype(jnp.float32), value_rows.astype(jnp.float32)).astype(jnp.bfloat16)

def finalize_output(tokens, shift_scale, mixed, w_proj):
    proj = jnp.dot(mixed.reshape(-1, D), w_proj, preferred_element_type=jnp.float32).reshape(tokens.shape)
    return (tokens.astype(jnp.float32) + shift_scale[2] * proj).astype(jnp.bfloat16)

def make_qkv(tokens, shift_scale, w_qkv, gains):
    normed = modulate(tokens, shift_scale)
    lead = tokens.shape[:-1]
    projected = jnp.dot(normed.reshape(-1, D), w_qkv, preferred_element_type=jnp.float32)
    return qk_normalize(projected.reshape(lead + (3, D)), gains)

def reference(tokens_a, modulate_a, spatial_qkv, spatial_proj, spatial_gain, tokens_b, modulation_rows_b, temporal_qkv, temporal_proj, temporal_gain):
    head_dim = D // HEADS
    qkv_a = make_qkv(tokens_a, modulate_a, spatial_qkv, spatial_gain)
    frames, spots = (tokens_a.shape[0], tokens_a.shape[1])

    def one_frame(frame_qkv):
        heads = frame_qkv.reshape(spots, 3, HEADS, head_dim).transpose(2, 1, 0, 3)
        outs = lax.map(lambda item: attend_long(item[0], item[1], item[2]), heads)
        return outs.transpose(1, 0, 2).reshape(spots, D)
    mixed_a = lax.map(one_frame, qkv_a)
    result_a = finalize_output(tokens_a, modulate_a, mixed_a, spatial_proj)
    qkv_b = make_qkv(tokens_b, modulation_rows_b, temporal_qkv, temporal_gain)
    heads_b = qkv_b.reshape(frames, spots, 3, HEADS, head_dim).transpose(3, 2, 1, 0, 4)
    outs_b = lax.map(lambda item: attend_frames(item[0], item[1], item[2]), heads_b)
    mixed_b = outs_b.transpose(2, 1, 0, 3).reshape(frames, spots, D)
    result_b = finalize_output(tokens_b, modulation_rows_b, mixed_b, temporal_proj)
    return (result_a, result_b)
```

```python
import functools
import math

import jax
import jax.numpy as jnp
from jax import lax
from jax.experimental import pallas as pl
from jax.experimental.pallas import tpu as pltpu
from jax.sharding import PartitionSpec as P

D = 1152
HEADS = 16
HD = 72
EXP_SCALE = math.log2(math.e) / math.sqrt(HD)
EPS = 1e-06
MESH = pl.DeviceIdType.MESH
F32 = jnp.float32
BF16 = jnp.bfloat16


def nt(a, b):
    return lax.dot_general(a, b, (((1,), (1,)), ((), ())), preferred_element_type=F32)


def nn(a, b):
    return lax.dot_general(a, b, (((1,), (0,)), ((), ())), preferred_element_type=F32)


def layer_norm(x, mod):
    center = x - jnp.mean(x, axis=-1, keepdims=True)
    spread = jnp.mean(center * center, axis=-1, keepdims=True)
    normed = center * lax.rsqrt(spread + EPS)
    return normed * (1.0 + mod[1:2, :]) + mod[0:1, :]


def head_norm(part, gain):
    p = part.reshape(part.shape[0] // HD, HD, part.shape[1])
    scale = lax.rsqrt(jnp.mean(p * p, axis=1, keepdims=True) + EPS)
    return p * scale * gain[None]


def gain_column(gain_row):
    rows = lax.broadcasted_iota(jnp.int32, (HD, HD), 0)
    cols = lax.broadcasted_iota(jnp.int32, (HD, HD), 1)
    return jnp.sum(jnp.where(rows == cols, gain_row, 0.0), axis=1, keepdims=True)


def with_ones(v):
    rows = lax.broadcasted_iota(jnp.int32, (8, v.shape[1]), 0)
    return jnp.concatenate([v, jnp.where(rows == 0, 1.0, 0.0)], axis=0).astype(BF16)


def kernel(
    ta, moda, wqa, wpa, ga, tb, modb, wqb, wpb, gb,
    ra, rb,
    ta_v, na, xa, xp, wa_raw, wt_tmp, wta, wb_raw, wtb, wpa_v, wpb_v,
    q_s, k_s, v_s, xb, nb, qb_s, kb_s, vb_s, mixb, rbs, mas, mx, ma_n, outa,
    sl, s_bt, r_bt, s_y, s_sib, s_x, r_x, r_xa, s_br, r_br, s_mx, r_mx,
):
    fi = lax.axis_index("frame")
    ri = lax.axis_index("row")
    y = ri // 4
    xh = (ri // 2) % 2
    c = ri % 2
    pair = y // 2
    my_f = 2 * pair + xh
    m = (y % 2) * 2 + c

    def row_dev(yy, hh, cc):
        return (fi, yy * 4 + hh * 2 + cc)

    sib = row_dev(y, xh, 1 - c)
    part_x = row_dev(y, 1 - xh, c)
    mate_y = 2 * pair + 1 - (y % 2)
    mate = row_dev(mate_y, xh, c)
    other_y = [2 * (1 - pair) + (y % 2), 2 * (1 - pair) + 1 - (y % 2)]
    others = [row_dev(yy, xh, c) for yy in other_y]
    r_part = y * 4 + (1 - xh) * 2 + c

    def remote(src, dst, ss, rs, dev):
        return pltpu.make_async_remote_copy(
            src_ref=src, dst_ref=dst, send_sem=ss, recv_sem=rs, device_id=dev, device_id_type=MESH
        )

    loads = {}

    def load(name, src, dst, k):
        loads[name] = pltpu.make_async_copy(src, dst, sl.at[k])
        loads[name].start()

    load("ta", ta, ta_v, 0)
    for part in range(3):
        start = pl.multiple_of(part * D + 256 * m, 128)
        load(("wa", part), wqa.at[:, pl.ds(start, 384)], wa_raw.at[part], 1 + part)
    load("wb", wqb, wb_raw, 4)
    load("wpa", wpa, wpa_v, 5)
    load("wpb", wpb, wpb_v, 6)
    load("tb", tb.at[:, pl.ds(pl.multiple_of(16 * fi, 16), 16), :], xb.at[fi], 7)

    barrier = pltpu.get_barrier_semaphore()
    for k in range(1, 16):
        pl.semaphore_signal(barrier, inc=1, device_id=(fi, (ri + k) % 16), device_id_type=MESH)
    for k in range(1, 8):
        pl.semaphore_signal(barrier, inc=1, device_id=((fi + k) % 8, ri), device_id_type=MESH)
    pl.semaphore_wait(barrier, 22)

    sends = []
    for k in range(1, 8):
        g = (fi + k) % 8
        cp = remote(
            tb.at[:, pl.ds(pl.multiple_of(16 * g, 16), 16), :],
            xb.at[fi], s_bt.at[k], r_bt.at[fi], (g, ri),
        )
        cp.start()
        sends.append(cp)

    loads["ta"].wait()

    def norm_frame(f, dst):
        dst[...] = layer_norm(ta_v[f].astype(F32), moda).astype(BF16)

    def start(src, dst, ss, rs, dev):
        cp = remote(src, dst, ss, rs, dev)
        cp.start()
        sends.append(cp)

    norm_frame(2 * (1 - pair) + xh, na.at[0])
    for k in range(2):
        start(na.at[0], xa.at[ri], s_y.at[k], r_xa.at[ri], others[k])
    norm_frame(2 * (1 - pair) + 1 - xh, na.at[1])
    start(na.at[1], xp, s_x.at[0], r_x, part_x)
    norm_frame(my_f, xa.at[ri])
    start(xa.at[ri], xa.at[ri], s_y.at[2], r_xa.at[ri], mate)
    start(xa.at[ri], xa.at[ri], s_sib.at[0], r_xa.at[ri], sib)
    norm_frame(2 * pair + 1 - xh, na.at[2])
    start(na.at[2], xa.at[ri], s_x.at[1], r_xa.at[ri], part_x)

    for part in range(3):
        loads[("wa", part)].wait()
        wt_tmp[...] = wa_raw[part].T
        wta[part * 288:(part + 1) * 288, :] = wt_tmp[pl.ds(pl.multiple_of(32 * m, 32), 288), :]
    loads["wb"].wait()

    @pl.loop(0, 27)
    def _(i):
        at = pl.multiple_of(i * 128, 128)
        wtb[pl.ds(at, 128), :] = wb_raw[:, pl.ds(at, 128)].T

    gain_a = [gain_column(ga[0:1, :]), gain_column(ga[1:2, :])]
    gain_b = [gain_column(gb[0:1, :]), gain_column(gb[1:2, :])]

    def arrived(yy, hh, cc, frm):
        r = yy * 4 + hh * 2 + cc
        remote(xa.at[r], xa.at[r], s_sib.at[0], r_xa.at[r], frm).wait_recv()

    def pass_on(k, yy, hh):
        r = yy * 4 + hh * 2 + c
        start(xa.at[r], xa.at[r], s_sib.at[k], r_xa.at[r], sib)

    arrived(mate_y, xh, c, mate)
    pass_on(1, mate_y, xh)
    for k in range(2):
        arrived(other_y[k], xh, c, others[k])
        pass_on(2 + k, other_y[k], xh)

    def norm_b(g):
        x = layer_norm(xb[g].astype(F32).reshape(64, D), modb).reshape(4, 2, 8, D)
        for half in range(2):
            nb[half, pl.ds(pl.multiple_of(g * 32, 32), 32), :] = (
                x[:, half].reshape(32, D).astype(BF16)
            )

    loads["tb"].wait()
    norm_b(fi)
    for k in range(1, 8):
        g = (fi + 8 - k) % 8
        remote(xb.at[g], xb.at[g], s_bt.at[0], r_bt.at[g], (g, ri)).wait_recv()
        norm_b(g)

    def qkv_b(half):
        x = nb[half]
        cols = slice(half * 256, half * 256 + 256)
        q = head_norm(nt(wtb[0:D, :], x), gain_b[0])
        for h in range(HEADS):
            qb_s[h, cols, :] = q[h].T.astype(BF16)
        kk = head_norm(nt(wtb[D:2 * D, :], x), gain_b[1])
        for h in range(HEADS):
            kb_s[h, :, cols] = kk[h].astype(BF16)
        v = nt(wtb[2 * D:3 * D, :], x)
        for h in range(HEADS):
            vb_s[h, :, cols] = with_ones(v[h * HD:(h + 1) * HD])

    qkv_b(0)
    remote(xp, xp, s_x.at[0], r_x, part_x).wait_recv()
    for k in range(2):
        start(xp, xa.at[r_part], s_y.at[3 + k], r_xa.at[r_part], others[k])
    qkv_b(1)
    arrived(y, 1 - xh, c, part_x)
    start(xa.at[r_part], xa.at[r_part], s_y.at[5], r_xa.at[r_part], mate)
    pass_on(4, y, 1 - xh)

    same = (
        lax.broadcasted_iota(jnp.int32, (256, 256), 0) % 8
        == lax.broadcasted_iota(jnp.int32, (256, 256), 1) % 8
    )

    @pl.loop(0, HEADS // 2)
    def _(hp):
        for half in range(2):
            cols = slice(half * 256, half * 256 + 256)
            outs = []
            for j in range(2):
                h = hp * 2 + j
                s = jnp.where(same, nn(qb_s[h, cols, :], kb_s[h, :, cols]), -1e30)
                top = jnp.max(s, axis=1, keepdims=True)
                p = jnp.exp2((s - top) * EXP_SCALE).astype(BF16)
                ot = nt(vb_s[h, :, cols], p)
                outs.append(ot[:HD] * (1.0 / ot[HD:HD + 1]))
            mixb[pl.ds(pl.multiple_of(hp * 144, 144), 144), cols] = (
                jnp.concatenate(outs, axis=0).astype(BF16)
            )

    arrived(mate_y, 1 - xh, c, mate)
    pass_on(5, mate_y, 1 - xh)

    loads["wpb"].wait()
    halves = []
    for half in range(2):
        proj = nn(mixb[:, half * 256:half * 256 + 256].T, wpb_v[...])
        halves.append((proj * modb[2:3, :]).reshape(32, 8, D))
    delta = jnp.concatenate([h[:, None] for h in halves], axis=1).reshape(8, 4, 16, D)
    rbs[...] = (xb[...].astype(F32) + delta).astype(BF16)

    for k in range(2):
        arrived(other_y[k], 1 - xh, c, others[k])
        pass_on(6 + k, other_y[k], 1 - xh)

    at_fi = pl.ds(pl.multiple_of(16 * fi, 16), 16)
    for k in range(1, 8):
        g = (fi + k) % 8
        start(rbs.at[g], rb.at[:, at_fi, :], s_br.at[k], r_br.at[fi], (g, ri))
    own_b = pltpu.make_async_copy(rbs.at[fi], rb.at[:, at_fi, :], s_br.at[0])
    own_b.start()

    def qkv_a(yy, hh):
        g = yy * 2 + hh
        x = xa[pl.ds(2 * g, 2)].reshape(256, D)
        rows = pl.ds(pl.multiple_of(g * 256, 256), 256)
        out = nt(wta[...], x)
        q = head_norm(out[0:288], gain_a[0])
        kk = head_norm(out[288:576], gain_a[1])
        for h in range(4):
            q_s[h, rows, :] = q[h].T.astype(BF16)
            k_s[h, :, rows] = kk[h].astype(BF16)
            v_s[h, :, rows] = with_ones(out[576 + h * HD:576 + (h + 1) * HD])

    for hh in (xh, 1 - xh):
        for yy in (y, mate_y, other_y[0], other_y[1]):
            arrived(yy, hh, 1 - c, sib)
            qkv_a(yy, hh)

    def scores(h, blk):
        return nn(q_s[h, pl.ds(pl.multiple_of(blk * 256, 256), 256), :], k_s[h])

    @pl.loop(0, 4)
    def _(i):
        b0 = 2 * ((i + my_f) % 4)
        items = [(b, h) for b in range(2) for h in range(4)]
        s = scores(items[0][1], b0)
        outs = []
        for n, (b, h) in enumerate(items):
            following = None
            if n + 1 < len(items):
                following = scores(items[n + 1][1], b0 + items[n + 1][0])
            top = jnp.max(s, axis=1, keepdims=True)
            p = jnp.exp2((s - top) * EXP_SCALE).astype(BF16)
            ot = nt(v_s[h], p)
            outs.append(ot[:HD] * (1.0 / ot[HD:HD + 1]))
            if h == 3:
                block = jnp.concatenate(outs, axis=0).astype(BF16)
                outs = []
                for cc in range(2):
                    r = (b0 + b) * 2 + cc
                    mas[r] = block[:, cc * 128:(cc + 1) * 128]
            s = following
        for k in range(4):
            r = b0 * 2 + k

            @pl.when(r != ri)
            def _():
                remote(
                    mas.at[r], mx.at[my_f, pl.ds(pl.multiple_of(288 * m, 32), 288), :],
                    s_mx.at[r], r_mx.at[my_f * 4 + m], (fi, r),
                ).start()

    own_m = pltpu.make_async_copy(
        mas.at[ri], mx.at[my_f, pl.ds(pl.multiple_of(288 * m, 32), 288), :], s_mx.at[ri]
    )
    own_m.start()
    own_m.wait()

    loads["wpa"].wait()
    for k in range(1, 16):
        r = (ri + k) % 16
        f_r = 2 * (r // 8) + (r // 2) % 2
        m_r = ((r // 4) % 2) * 2 + r % 2
        slot = mx.at[f_r, pl.ds(pl.multiple_of(288 * m_r, 32), 288), :]
        remote(slot, slot, s_mx.at[r], r_mx.at[f_r * 4 + m_r], (fi, r)).wait_recv()
    for f in range(4):
        ma_n[f * 128:(f + 1) * 128, :] = mx[f].T
    proj = nn(ma_n[...], wpa_v[...]).reshape(4, 128, D)
    outa[...] = (ta_v[...].astype(F32) + moda[2:3, :] * proj).astype(BF16)
    out_copy = pltpu.make_async_copy(outa, ra, sl.at[0])
    out_copy.start()

    for k in range(1, 8):
        g = (fi + k) % 8
        at_g = pl.ds(pl.multiple_of(16 * g, 16), 16)
        remote(rbs.at[g], rb.at[:, at_g, :], s_br.at[0], r_br.at[g], (g, ri)).wait_recv()
    for cp in sends:
        cp.wait_send()
    for k in range(1, 16):
        r = (ri + k) % 16
        remote(mas.at[r], mas.at[r], s_mx.at[r], r_mx.at[0], (fi, r)).wait_send()
    own_b.wait()
    out_copy.wait()


def per_device(*args):
    any_spec = pl.BlockSpec(memory_space=pl.ANY)
    vmem = pl.BlockSpec(memory_space=pltpu.VMEM)
    v = pltpu.VMEM
    dma = pltpu.SemaphoreType.DMA
    shape = jax.ShapeDtypeStruct((4, 128, D), BF16)
    specs = [any_spec, vmem, any_spec, any_spec, vmem]
    return pl.pallas_call(
        kernel,
        out_shape=(shape, shape),
        in_specs=specs + specs,
        out_specs=(any_spec, any_spec),
        scratch_shapes=[
            v((4, 128, D), BF16),
            v((3, 128, D), BF16),
            v((16, 128, D), BF16),
            v((128, D), BF16),
            v((3, D, 384), BF16),
            v((384, D), BF16),
            v((864, D), BF16),
            v((D, 3 * D), BF16),
            v((3 * D, D), BF16),
            v((D, D), BF16),
            v((D, D), BF16),
            v((4, 2048, HD), BF16),
            v((4, HD, 2048), BF16),
            v((4, 80, 2048), BF16),
            v((8, 4, 16, D), BF16),
            v((2, 256, D), BF16),
            v((HEADS, 512, HD), BF16),
            v((HEADS, HD, 512), BF16),
            v((HEADS, 80, 512), BF16),
            v((D, 512), BF16),
            v((8, 4, 16, D), BF16),
            v((16, 288, 128), BF16),
            v((4, D, 128), BF16),
            v((512, D), BF16),
            v((4, 128, D), BF16),
            dma((8,)),
            dma((8,)),
            dma((8,)),
            dma((6,)),
            dma((8,)),
            dma((2,)),
            dma,
            dma((16,)),
            dma((8,)),
            dma((8,)),
            dma((16,)),
            dma((16,)),
        ],
        compiler_params=pltpu.CompilerParams(
            collective_id=0, has_side_effects=True, vmem_limit_bytes=63 << 20
        ),
        cost_estimate=pl.CostEstimate(
            flops=25_000_000_000, bytes_accessed=40_000_000, transcendentals=20_000_000
        ),
    )(*args)


def solution(mesh):
    tokens = P("frame", "row", None)
    return jax.shard_map(
        per_device,
        mesh=mesh,
        in_specs=(tokens, P(), P(), P(), P(), tokens, P(), P(), P(), P()),
        out_specs=(tokens, tokens),
        check_vma=False,
    )
```

```python
import functools
import math

import jax
import jax.numpy as jnp
from jax import lax
from jax.experimental import pallas as pl
from jax.experimental.pallas import tpu as pltpu
from jax.sharding import PartitionSpec as P

D = 1152
HEADS = 16
HD = 72
EXP_SCALE = math.log2(math.e) / math.sqrt(HD)
EPS = 1e-06
MESH = pl.DeviceIdType.MESH
F32 = jnp.float32
BF16 = jnp.bfloat16


def nt(a, b):
    return lax.dot_general(a, b, (((1,), (1,)), ((), ())), preferred_element_type=F32)


def nn(a, b):
    return lax.dot_general(a, b, (((1,), (0,)), ((), ())), preferred_element_type=F32)


def layer_norm(x, mod):
    center = x - jnp.mean(x, axis=-1, keepdims=True)
    spread = jnp.mean(center * center, axis=-1, keepdims=True)
    normed = center * lax.rsqrt(spread + EPS)
    return normed * (1.0 + mod[1:2, :]) + mod[0:1, :]


def head_norm(part, gain):
    p = part.reshape(part.shape[0] // HD, HD, part.shape[1])
    scale = lax.rsqrt(jnp.mean(p * p, axis=1, keepdims=True) + EPS)
    return p * scale * gain[None]


def gain_column(gain_row):
    rows = lax.broadcasted_iota(jnp.int32, (HD, HD), 0)
    cols = lax.broadcasted_iota(jnp.int32, (HD, HD), 1)
    return jnp.sum(jnp.where(rows == cols, gain_row, 0.0), axis=1, keepdims=True)


def with_ones(v):
    rows = lax.broadcasted_iota(jnp.int32, (8, v.shape[1]), 0)
    return jnp.concatenate([v, jnp.where(rows == 0, 1.0, 0.0)], axis=0).astype(BF16)


def kernel(
    ta, moda, wqa, wpa, ga, tb, modb, wqb, wpb, gb,
    ra, rb,
    ta_v, tb_v, na, xa, wa_raw, wt_tmp, wta, wb_raw, wtb, wpa_v, wpb_v,
    q_s, k_s, v_s, xb, nb, qb_s, kb_s, vb_s, mixb, rbs, mas, mx, ma_n,
    sl, s_bt, r_bt, s_d, s_mate, s_sib, r_xa, s_br, r_br, s_mx, r_mx,
):
    fi = lax.axis_index("frame")
    ri = lax.axis_index("row")
    y = ri // 4
    xh = (ri // 2) % 2
    c = ri % 2
    pair = y // 2
    my_f = 2 * pair + xh
    m = (y % 2) * 2 + c

    def row_dev(yy, hh, cc):
        return (fi, yy * 4 + hh * 2 + cc)

    sib = row_dev(y, xh, 1 - c)
    mate_y = 2 * pair + 1 - (y % 2)
    mate = row_dev(mate_y, xh, c)
    across_y = 3 - y
    mate_across_y = 3 - mate_y

    def remote(src, dst, ss, rs, dev):
        return pltpu.make_async_remote_copy(
            src_ref=src, dst_ref=dst, send_sem=ss, recv_sem=rs, device_id=dev, device_id_type=MESH
        )

    loads = {}

    def load(name, src, dst, k):
        loads[name] = pltpu.make_async_copy(src, dst, sl.at[k])
        loads[name].start()

    load("tb", tb, tb_v, 7)
    load("ta", ta, ta_v, 0)
    for part in range(3):
        first = pl.multiple_of(part * D + 256 * m, 128)
        load(("wa", part), wqa.at[:, pl.ds(first, 384)], wa_raw.at[part], 1 + part)
    load("wb", wqb, wb_raw, 4)
    load("wpa", wpa, wpa_v, 5)
    load("wpb", wpb, wpb_v, 6)

    barrier = pltpu.get_barrier_semaphore()
    near = [sib, mate, row_dev(across_y, xh, c), row_dev(y, 1 - xh, c), row_dev(across_y, 1 - xh, c)]
    near += [((fi + k) % 8, ri) for k in range(1, 8)]
    for device in near:
        pl.semaphore_signal(barrier, inc=1, device_id=device, device_id_type=MESH)
    pl.semaphore_wait(barrier, len(near))

    sends = []
    loads["tb"].wait()
    for k in range(1, 8):
        g = (fi + k) % 8
        cp = remote(
            tb_v.at[:, pl.ds(pl.multiple_of(16 * g, 16), 16), :],
            xb.at[fi], s_bt.at[k], r_bt.at[fi], (g, ri),
        )
        cp.start()
        sends.append(cp)

    loads["ta"].wait()

    def norm_frame(f, dst):
        dst[...] = layer_norm(ta_v[f].astype(F32), moda).astype(BF16)

    def start(src, dst, ss, rs, dev):
        cp = remote(src, dst, ss, rs, dev)
        cp.start()
        sends.append(cp)

    norm_frame(2 * (1 - pair) + xh, na.at[0])
    start(na.at[0], xa.at[ri], s_d.at[0], r_xa.at[ri, 0], row_dev(across_y, xh, c))
    norm_frame(my_f, xa.at[ri])
    start(xa.at[ri], xa.at[ri], s_mate.at[0, 0], r_xa.at[ri, 0], mate)
    start(xa.at[ri], xa.at[ri], s_sib.at[0, 0], r_xa.at[ri, 0], sib)
    norm_frame(2 * (1 - pair) + 1 - xh, na.at[1])
    norm_frame(2 * pair + 1 - xh, na.at[2])

    whole = ((0, 128),)
    in_halves = ((0, 64), (64, 64))

    def piece(r, k, part):
        return xa.at[r, pl.ds(*part), :], r_xa.at[r, k]

    def arrived(yy, hh, cc, frm, parts=whole):
        r = yy * 4 + hh * 2 + cc
        for k, part in enumerate(parts):
            ref, sem = piece(r, k, part)
            remote(ref, ref, s_sib.at[0, 0], sem, frm).wait_recv()

    def pass_on(yy, hh, frm, targets, parts=whole):
        r = yy * 4 + hh * 2 + c
        for k, part in enumerate(parts):
            ref, sem = piece(r, k, part)
            remote(ref, ref, s_sib.at[0, 0], sem, frm).wait_recv()
            for send_sem, device in targets:
                start(ref, ref, send_sem.at[k], sem, device)

    def from_source(n, yy, hh, parts=whole):
        targets = ((s_mate.at[n], mate), (s_sib.at[n], sib))
        pass_on(yy, hh, row_dev(yy, hh, c), targets, parts)

    def from_mate(n, yy, hh, parts=whole):
        pass_on(yy, hh, mate, ((s_sib.at[n], sib),), parts)

    for part in range(3):
        loads[("wa", part)].wait()
        wt_tmp[...] = wa_raw[part].T
        wta[part * 288:(part + 1) * 288, :] = wt_tmp[pl.ds(pl.multiple_of(32 * m, 32), 288), :]
    from_source(1, across_y, xh)
    from_mate(4, mate_y, xh)
    loads["wb"].wait()

    @pl.loop(0, 27)
    def _(i):
        at = pl.multiple_of(i * 128, 128)
        wtb[pl.ds(at, 128), :] = wb_raw[:, pl.ds(at, 128)].T

    gain_a = [gain_column(ga[0:1, :]), gain_column(ga[1:2, :])]
    gain_b = [gain_column(gb[0:1, :]), gain_column(gb[1:2, :])]

    def qkv_a(yy, hh):
        g = yy * 2 + hh
        x = xa[pl.ds(2 * g, 2)].reshape(256, D)
        rows = pl.ds(pl.multiple_of(g * 256, 256), 256)
        out = nt(wta[...], x)
        q = head_norm(out[0:288], gain_a[0])
        kk = head_norm(out[288:576], gain_a[1])
        for h in range(4):
            q_s[h, rows, :] = q[h].T.astype(BF16)
            k_s[h, :, rows] = kk[h].astype(BF16)
            v_s[h, :, rows] = with_ones(out[576 + h * HD:576 + (h + 1) * HD])

    def group_a(yy, hh, parts=whole):
        arrived(yy, hh, 1 - c, sib, parts)
        qkv_a(yy, hh)

    group_a(y, xh)
    group_a(mate_y, xh)
    group_a(across_y, xh)

    def norm_b(g):
        x = layer_norm(xb[g].astype(F32).reshape(64, D), modb).reshape(4, 2, 8, D)
        for half in range(2):
            nb[half, pl.ds(pl.multiple_of(g * 32, 32), 32), :] = (
                x[:, half].reshape(32, D).astype(BF16)
            )

    xb[fi] = tb_v[:, pl.ds(pl.multiple_of(16 * fi, 16), 16), :]
    norm_b(fi)
    for k in range(1, 8):
        g = (fi + 8 - k) % 8
        remote(xb.at[g], xb.at[g], s_bt.at[0], r_bt.at[g], (g, ri)).wait_recv()
        norm_b(g)

    def qkv_b(half):
        x = nb[half]
        cols = slice(half * 256, half * 256 + 256)
        q = head_norm(nt(wtb[0:D, :], x), gain_b[0])
        for h in range(HEADS):
            qb_s[h, cols, :] = q[h].T.astype(BF16)
        kk = head_norm(nt(wtb[D:2 * D, :], x), gain_b[1])
        for h in range(HEADS):
            kb_s[h, :, cols] = kk[h].astype(BF16)
        v = nt(wtb[2 * D:3 * D, :], x)
        for h in range(HEADS):
            vb_s[h, :, cols] = with_ones(v[h * HD:(h + 1) * HD])

    start(na.at[1], xa.at[ri], s_d.at[1], r_xa.at[ri, 0], row_dev(across_y, 1 - xh, c))
    from_mate(5, mate_across_y, xh)
    qkv_b(0)
    qkv_b(1)
    for k, part in enumerate(in_halves):
        start(
            na.at[2, pl.ds(*part), :], xa.at[ri, pl.ds(*part), :], s_d.at[2 + k], r_xa.at[ri, k],
            row_dev(y, 1 - xh, c),
        )

    same = (
        lax.broadcasted_iota(jnp.int32, (256, 256), 0) % 8
        == lax.broadcasted_iota(jnp.int32, (256, 256), 1) % 8
    )

    def attend_b(hp):
        blocks = [(j, half) for j in range(2) for half in range(2)]
        cols = [slice(0, 256), slice(256, 512)]
        ss = [
            jnp.where(same, nn(qb_s[hp * 2 + j, cols[half], :], kb_s[hp * 2 + j, :, cols[half]]), -1e30)
            for j, half in blocks
        ]
        tops = [jnp.max(s, axis=1, keepdims=True) for s in ss]
        ps = [jnp.exp2((s - top) * EXP_SCALE).astype(BF16) for s, top in zip(ss, tops)]
        ots = [nt(vb_s[hp * 2 + j, :, cols[half]], p) for (j, half), p in zip(blocks, ps)]
        ots = [ot[:HD] * (1.0 / ot[HD:HD + 1]) for ot in ots]
        for half in range(2):
            mixb[pl.ds(pl.multiple_of(hp * 144, 144), 144), cols[half]] = (
                jnp.concatenate([ots[half], ots[2 + half]], axis=0).astype(BF16)
            )

    pl.loop(0, 4)(attend_b)
    from_source(2, across_y, 1 - xh)
    pl.loop(4, 8)(attend_b)
    loads["wpb"].wait()
    halves = []
    for half in range(2):
        proj = nn(mixb[:, half * 256:half * 256 + 256].T, wpb_v[...])
        halves.append((proj * modb[2:3, :]).reshape(32, 8, D))
    delta = jnp.concatenate([h[:, None] for h in halves], axis=1).reshape(8, 4, 16, D)
    rbs[...] = (xb[...].astype(F32) + delta).astype(BF16)

    group_a(mate_across_y, xh)
    from_source(3, y, 1 - xh, in_halves)
    at_fi = pl.ds(pl.multiple_of(16 * fi, 16), 16)
    for k in range(1, 8):
        g = (fi + k) % 8
        start(rbs.at[g], rb.at[:, at_fi, :], s_br.at[k], r_br.at[fi], (g, ri))
    own_b = pltpu.make_async_copy(rbs.at[fi], rb.at[:, at_fi, :], s_br.at[0])
    own_b.start()

    from_mate(6, mate_across_y, 1 - xh)
    group_a(across_y, 1 - xh)
    group_a(mate_across_y, 1 - xh)
    group_a(y, 1 - xh, in_halves)
    from_mate(7, mate_y, 1 - xh, in_halves)
    group_a(mate_y, 1 - xh, in_halves)

    def scores(h, blk):
        return nn(q_s[h, pl.ds(pl.multiple_of(blk * 256, 256), 256), :], k_s[h])

    my_slot = mx.at[my_f, pl.ds(pl.multiple_of(288 * m, 32), 288), :]

    def send_mixed(r):
        @pl.when(r != ri)
        def _():
            remote(mas.at[r], my_slot, s_mx.at[r], r_mx.at[my_f * 4 + m], (fi, r)).start()

    @pl.loop(0, 4)
    def _(i):
        b0 = 2 * ((i + my_f) % 4)
        items = [(b, h) for b in range(2) for h in range(4)]
        s = scores(items[0][1], b0)
        outs = []
        for n, (b, h) in enumerate(items):
            following = None
            if n + 1 < len(items):
                following = scores(items[n + 1][1], b0 + items[n + 1][0])
            top = jnp.max(s, axis=1, keepdims=True)
            p = jnp.exp2((s - top) * EXP_SCALE).astype(BF16)
            ot = nt(v_s[h], p)
            outs.append(ot[:HD] * (1.0 / ot[HD:HD + 1]))
            if h == 3:
                block = jnp.concatenate(outs, axis=0).astype(BF16)
                outs = []
                for cc in range(2):
                    r = (b0 + b) * 2 + cc
                    mas[r] = block[:, cc * 128:(cc + 1) * 128]
                for cc in range(2):
                    send_mixed((b0 + b) * 2 + cc)
            s = following

    own_m = pltpu.make_async_copy(mas.at[ri], my_slot, s_mx.at[ri])
    own_m.start()
    own_m.wait()

    loads["wpa"].wait()

    def project(frames):
        for n, f in enumerate(frames):
            for mm in range(4):
                r = (2 * (f // 2) + mm // 2) * 4 + (f % 2) * 2 + mm % 2

                @pl.when(r != ri)
                def _():
                    slot = mx.at[f, mm * 288:(mm + 1) * 288, :]
                    remote(slot, slot, s_mx.at[r], r_mx.at[f * 4 + mm], (fi, r)).wait_recv()
            ma_n[n * 128:(n + 1) * 128, :] = mx[f].T
        proj = nn(ma_n[:len(frames) * 128, :], wpa_v[...])
        for n, f in enumerate(frames):
            delta = moda[2:3, :] * proj[n * 128:(n + 1) * 128]
            ra[f] = (ta_v[f].astype(F32) + delta).astype(BF16)

    order = [(ri // 4 + 4 - n) % 4 for n in range(4)]
    project(order[:3])
    project(order[3:])

    for k in range(1, 8):
        g = (fi + k) % 8
        at_g = pl.ds(pl.multiple_of(16 * g, 16), 16)
        remote(rbs.at[g], rb.at[:, at_g, :], s_br.at[0], r_br.at[g], (g, ri)).wait_recv()
    for cp in sends:
        cp.wait_send()
    for k in range(1, 16):
        r = (ri + k) % 16
        remote(mas.at[r], mas.at[r], s_mx.at[r], r_mx.at[0], (fi, r)).wait_send()
    own_b.wait()


def per_device(*args):
    any_spec = pl.BlockSpec(memory_space=pl.ANY)
    vmem = pl.BlockSpec(memory_space=pltpu.VMEM)
    v = pltpu.VMEM
    dma = pltpu.SemaphoreType.DMA
    specs = [any_spec, vmem, any_spec, any_spec, vmem]
    return pl.pallas_call(
        kernel,
        out_shape=(v((4, 128, D), BF16), v((4, 128, D), BF16)),
        in_specs=specs + specs,
        out_specs=(vmem, vmem),
        scratch_shapes=[
            v((4, 128, D), BF16),
            v((4, 128, D), BF16),
            v((3, 128, D), BF16),
            v((16, 128, D), BF16),
            v((3, D, 384), BF16),
            v((384, D), BF16),
            v((864, D), BF16),
            v((D, 3 * D), BF16),
            v((3 * D, D), BF16),
            v((D, D), BF16),
            v((D, D), BF16),
            v((4, 2048, HD), BF16),
            v((4, HD, 2048), BF16),
            v((4, 80, 2048), BF16),
            v((8, 4, 16, D), BF16),
            v((2, 256, D), BF16),
            v((HEADS, 512, HD), BF16),
            v((HEADS, HD, 512), BF16),
            v((HEADS, 80, 512), BF16),
            v((D, 512), BF16),
            v((8, 4, 16, D), BF16),
            v((16, 288, 128), BF16),
            v((4, D, 128), BF16),
            v((512, D), BF16),
            dma((8,)),
            dma((8,)),
            dma((8,)),
            dma((4,)),
            dma((4, 2)),
            dma((8, 2)),
            dma((16, 2)),
            dma((8,)),
            dma((8,)),
            dma((16,)),
            dma((16,)),
        ],
        compiler_params=pltpu.CompilerParams(
            collective_id=0, has_side_effects=True, vmem_limit_bytes=60 << 20
        ),
        cost_estimate=pl.CostEstimate(
            flops=25_000_000_000, bytes_accessed=40_000_000, transcendentals=20_000_000
        ),
    )(*args)


def solution(mesh):
    tokens = P("frame", "row", None)
    return jax.shard_map(
        per_device,
        mesh=mesh,
        in_specs=(tokens, P(), P(), P(), P(), tokens, P(), P(), P(), P()),
        out_specs=(tokens, tokens),
        check_vma=False,
    )
```

```python
import functools
import math

import jax
import jax.numpy as jnp
from jax import lax
from jax.experimental import pallas as pl
from jax.experimental.pallas import tpu as pltpu
from jax.sharding import PartitionSpec as P

D = 1152
HEADS = 16
HD = 72
EXP_SCALE = math.log2(math.e) / math.sqrt(HD)
EPS = 1e-06
MESH = pl.DeviceIdType.MESH
F32 = jnp.float32
BF16 = jnp.bfloat16


def nt(a, b):
    return lax.dot_general(a, b, (((1,), (1,)), ((), ())), preferred_element_type=F32)


def nn(a, b):
    return lax.dot_general(a, b, (((1,), (0,)), ((), ())), preferred_element_type=F32)


def layer_norm(x, mod):
    center = x - jnp.mean(x, axis=-1, keepdims=True)
    spread = jnp.mean(center * center, axis=-1, keepdims=True)
    normed = center * lax.rsqrt(spread + EPS)
    return normed * (1.0 + mod[1:2, :]) + mod[0:1, :]


def head_norm(part, gain):
    p = part.reshape(part.shape[0] // HD, HD, part.shape[1])
    scale = lax.rsqrt(jnp.mean(p * p, axis=1, keepdims=True) + EPS)
    return p * scale * gain[None]


def gain_column(gain_row):
    rows = lax.broadcasted_iota(jnp.int32, (HD, HD), 0)
    cols = lax.broadcasted_iota(jnp.int32, (HD, HD), 1)
    return jnp.sum(jnp.where(rows == cols, gain_row, 0.0), axis=1, keepdims=True)


def with_ones(v):
    rows = lax.broadcasted_iota(jnp.int32, (8, v.shape[1]), 0)
    return jnp.concatenate([v, jnp.where(rows == 0, 1.0, 0.0)], axis=0).astype(BF16)


def kernel(
    ta, moda, wqa, wpa, ga, tb, modb, wqb, wpb, gb,
    ra, rb,
    ta_v, tb_v, na, xa, wa_raw, wt_tmp, wta, wb_raw, wtb, wpa_v, wpb_v,
    q_s, k_s, v_s, part_out, tops, xb, nb, qb_s, kb_s, vb_s, mixb, rbs, mas, mx, ma_n,
    sl, s_wb, s_bt, r_bt, s_d, s_mate, s_sib, r_xa, s_br, r_br, s_mx, r_mx,
):
    fi = lax.axis_index("frame")
    ri = lax.axis_index("row")
    y = ri // 4
    xh = (ri // 2) % 2
    c = ri % 2
    pair = y // 2
    my_f = 2 * pair + xh
    m = (y % 2) * 2 + c

    def row_dev(yy, hh, cc):
        return (fi, yy * 4 + hh * 2 + cc)

    sib = row_dev(y, xh, 1 - c)
    mate_y = 2 * pair + 1 - (y % 2)
    mate = row_dev(mate_y, xh, c)
    across_y = 3 - y
    mate_across_y = 3 - mate_y

    def remote(src, dst, ss, rs, dev):
        return pltpu.make_async_remote_copy(
            src_ref=src, dst_ref=dst, send_sem=ss, recv_sem=rs, device_id=dev, device_id_type=MESH
        )

    loads = {}

    def load(name, src, dst, k):
        loads[name] = pltpu.make_async_copy(src, dst, sl.at[k])
        loads[name].start()

    load("tb", tb, tb_v, 7)
    load("ta", ta, ta_v, 0)

    barrier = pltpu.get_barrier_semaphore()
    near = [sib, mate, row_dev(across_y, xh, c), row_dev(y, 1 - xh, c), row_dev(across_y, 1 - xh, c)]
    near += [((fi + k) % 8, ri) for k in range(1, 8)]
    for device in near:
        pl.semaphore_signal(barrier, inc=1, device_id=device, device_id_type=MESH)
    pl.semaphore_wait(barrier, len(near))

    sends = []
    loads["tb"].wait()
    for k in range(1, 8):
        g = (fi + k) % 8
        cp = remote(
            tb_v.at[:, pl.ds(pl.multiple_of(16 * g, 16), 16), :],
            xb.at[fi], s_bt.at[k], r_bt.at[fi], (g, ri),
        )
        cp.start()
        sends.append(cp)

    loads["ta"].wait()

    def norm_frame(f, dst):
        dst[...] = layer_norm(ta_v[f].astype(F32), moda).astype(BF16)

    def start(src, dst, ss, rs, dev):
        cp = remote(src, dst, ss, rs, dev)
        cp.start()
        sends.append(cp)

    norm_frame(2 * (1 - pair) + xh, na.at[0])
    start(na.at[0], xa.at[ri], s_d.at[0], r_xa.at[ri, 0], row_dev(across_y, xh, c))
    norm_frame(my_f, xa.at[ri])
    start(xa.at[ri], xa.at[ri], s_mate.at[0, 0], r_xa.at[ri, 0], mate)
    start(xa.at[ri], xa.at[ri], s_sib.at[0, 0], r_xa.at[ri, 0], sib)
    norm_frame(2 * (1 - pair) + 1 - xh, na.at[1])
    for part in range(3):
        first = pl.multiple_of(part * D + 256 * m, 128)
        load(("wa", part), wqa.at[:, pl.ds(first, 384)], wa_raw.at[part], 1 + part)
    def load_b(k, slot):
        return pltpu.make_async_copy(
            wqb.at[:, pl.ds(pl.multiple_of(k * 384, 128), 384)], wb_raw.at[slot], s_wb.at[slot]
        )

    for k in range(3):
        load_b(k, k).start()
    load("wpa", wpa, wpa_v, 5)
    load("wpb", wpb, wpb_v, 6)
    norm_frame(2 * pair + 1 - xh, na.at[2])

    whole = ((0, 128),)
    in_halves = ((0, 64), (64, 64))

    def piece(r, k, part):
        return xa.at[r, pl.ds(*part), :], r_xa.at[r, k]

    def arrived(yy, hh, cc, frm, parts=whole):
        r = yy * 4 + hh * 2 + cc
        for k, part in enumerate(parts):
            ref, sem = piece(r, k, part)
            remote(ref, ref, s_sib.at[0, 0], sem, frm).wait_recv()

    def pass_on(yy, hh, frm, targets, parts=whole, first=0):
        r = yy * 4 + hh * 2 + c
        for k, part in enumerate(parts, first):
            ref, sem = piece(r, k, part)
            remote(ref, ref, s_sib.at[0, 0], sem, frm).wait_recv()
            for send_sem, device in targets:
                start(ref, ref, send_sem.at[k], sem, device)

    def from_source(n, yy, hh, parts=whole, first=0):
        targets = ((s_mate.at[n], mate), (s_sib.at[n], sib))
        pass_on(yy, hh, row_dev(yy, hh, c), targets, parts, first)

    def from_mate(n, yy, hh, parts=whole, first=0):
        pass_on(yy, hh, mate, ((s_sib.at[n], sib),), parts, first)

    for part in range(3):
        loads[("wa", part)].wait()
        wt_tmp[...] = wa_raw[part].T
        wta[part * 288:(part + 1) * 288, :] = wt_tmp[pl.ds(pl.multiple_of(32 * m, 32), 288), :]
    from_source(1, across_y, xh)
    from_mate(4, mate_y, xh)

    @pl.loop(0, 9)
    def _(k):
        slot = k % 3
        load_b(k, slot).wait()
        for tile in range(3):
            at = pl.multiple_of(k * 384 + tile * 128, 128)
            wtb[pl.ds(at, 128), :] = wb_raw[slot, :, tile * 128:(tile + 1) * 128].T

        @pl.when(k < 6)
        def _():
            load_b(k + 3, slot).start()

    gain_a = [gain_column(ga[0:1, :]), gain_column(ga[1:2, :])]
    gain_b = [gain_column(gb[0:1, :]), gain_column(gb[1:2, :])]

    def qkv_a(yy, hh):
        g = yy * 2 + hh
        cols = pl.ds(pl.multiple_of((0 if hh is xh else 1024) + yy * 256, 256), 256)
        x = xa[pl.ds(2 * g, 2)].reshape(256, D)
        rows = pl.ds(pl.multiple_of(g * 256, 256), 256)
        out = nt(wta[...], x)
        q = head_norm(out[0:288], gain_a[0])
        kk = head_norm(out[288:576], gain_a[1])
        for h in range(4):
            q_s[h, rows, :] = q[h].T.astype(BF16)
            k_s[h, :, cols] = kk[h].astype(BF16)
            v_s[h, :, cols] = with_ones(out[576 + h * HD:576 + (h + 1) * HD])

    def group_a(yy, hh, parts=whole):
        arrived(yy, hh, 1 - c, sib, parts)
        qkv_a(yy, hh)

    group_a(y, xh)
    group_a(mate_y, xh)
    group_a(across_y, xh)

    def norm_b(g):
        x = layer_norm(xb[g].astype(F32).reshape(64, D), modb).reshape(4, 2, 8, D)
        for half in range(2):
            nb[half, pl.ds(pl.multiple_of(g * 32, 32), 32), :] = (
                x[:, half].reshape(32, D).astype(BF16)
            )

    xb[fi] = tb_v[:, pl.ds(pl.multiple_of(16 * fi, 16), 16), :]
    norm_b(fi)
    for k in range(1, 8):
        g = (fi + 8 - k) % 8
        remote(xb.at[g], xb.at[g], s_bt.at[0], r_bt.at[g], (g, ri)).wait_recv()
        norm_b(g)

    def send_half(k):
        part = in_halves[k]
        start(
            na.at[2, pl.ds(*part), :], xa.at[ri, pl.ds(*part), :], s_d.at[2 + k], r_xa.at[ri, k],
            row_dev(y, 1 - xh, c),
        )

    def qkv_b(half):
        x = nb[half]
        cols = slice(half * 256, half * 256 + 256)
        q = head_norm(nt(wtb[0:D, :], x), gain_b[0])
        for h in range(HEADS):
            qb_s[h, cols, :] = q[h].T.astype(BF16)
        kk = head_norm(nt(wtb[D:2 * D, :], x), gain_b[1])
        for h in range(HEADS):
            kb_s[h, :, cols] = kk[h].astype(BF16)
        v = nt(wtb[2 * D:3 * D, :], x)
        for h in range(HEADS):
            vb_s[h, :, cols] = with_ones(v[h * HD:(h + 1) * HD])

    start(na.at[1], xa.at[ri], s_d.at[1], r_xa.at[ri, 0], row_dev(across_y, 1 - xh, c))
    from_mate(5, mate_across_y, xh)
    qkv_b(0)
    qkv_b(1)
    send_half(0)

    same = (
        lax.broadcasted_iota(jnp.int32, (256, 256), 0) % 8
        == lax.broadcasted_iota(jnp.int32, (256, 256), 1) % 8
    )

    def attend_b(hp):
        blocks = [(j, half) for j in range(2) for half in range(2)]
        cols = [slice(0, 256), slice(256, 512)]
        ss = [
            jnp.where(same, nn(qb_s[hp * 2 + j, cols[half], :], kb_s[hp * 2 + j, :, cols[half]]), -1e30)
            for j, half in blocks
        ]
        tops = [jnp.max(s, axis=1, keepdims=True) for s in ss]
        ps = [jnp.exp2((s - top) * EXP_SCALE).astype(BF16) for s, top in zip(ss, tops)]
        ots = [nt(vb_s[hp * 2 + j, :, cols[half]], p) for (j, half), p in zip(blocks, ps)]
        ots = [ot[:HD] * (1.0 / ot[HD:HD + 1]) for ot in ots]
        for half in range(2):
            mixb[pl.ds(pl.multiple_of(hp * 144, 144), 144), cols[half]] = (
                jnp.concatenate([ots[half], ots[2 + half]], axis=0).astype(BF16)
            )

    pl.loop(0, 4)(attend_b)
    send_half(1)
    from_source(2, across_y, 1 - xh)
    pl.loop(4, 8)(attend_b)

    loads["wpb"].wait()
    halves = []
    for half in range(2):
        proj = nn(mixb[:, half * 256:half * 256 + 256].T, wpb_v[...])
        halves.append((proj * modb[2:3, :]).reshape(32, 8, D))
    delta = jnp.concatenate([h[:, None] for h in halves], axis=1).reshape(8, 4, 16, D)
    rbs[...] = (xb[...].astype(F32) + delta).astype(BF16)

    group_a(mate_across_y, xh)
    from_mate(6, mate_across_y, 1 - xh)

    def first_part(yy):
        rows = pl.ds(pl.multiple_of((yy * 2 + xh) * 256, 256), 256)

        def near_scores(h):
            return nn(q_s[h, rows, :], k_s[h, :, :1024])

        s = near_scores(0)
        for h in range(4):
            following = near_scores(h + 1) if h < 3 else None
            top = jnp.max(s, axis=1, keepdims=True)
            tops[yy, h] = top
            p = jnp.exp2((s - top) * EXP_SCALE).astype(BF16)
            part_out[yy, h] = nt(v_s[h, :, :1024], p)
            s = following

    pl.loop(0, 1)(first_part)
    from_source(3, y, 1 - xh, in_halves)
    at_fi = pl.ds(pl.multiple_of(16 * fi, 16), 16)
    for k in range(1, 8):
        g = (fi + k) % 8
        start(rbs.at[g], rb.at[:, at_fi, :], s_br.at[k], r_br.at[fi], (g, ri))
    own_b = pltpu.make_async_copy(rbs.at[fi], rb.at[:, at_fi, :], s_br.at[0])
    own_b.start()
    group_a(across_y, 1 - xh)
    pl.loop(1, 3)(first_part)
    from_mate(7, mate_y, 1 - xh, in_halves[:1], 0)
    pl.loop(3, 4)(first_part)
    group_a(mate_across_y, 1 - xh)
    from_mate(7, mate_y, 1 - xh, in_halves[1:], 1)
    group_a(y, 1 - xh, in_halves)
    group_a(mate_y, 1 - xh, in_halves)

    my_slot = mx.at[my_f, pl.ds(pl.multiple_of(288 * m, 32), 288), :]

    def send_mixed(r):
        @pl.when(r != ri)
        def _():
            remote(mas.at[r], my_slot, s_mx.at[r], r_mx.at[my_f * 4 + m], (fi, r)).start()

    @pl.loop(0, 4)
    def _(i):
        yy = (i + my_f) % 4
        blocks = [yy * 2 + 1 - xh, yy * 2 + xh]
        items = [(b, h) for b in range(2) for h in range(4)]

        def scores(b, h):
            q = q_s[h, pl.ds(pl.multiple_of(blocks[b] * 256, 256), 256), :]
            return nn(q, k_s[h, :, 1024:] if b == 1 else k_s[h])

        s = scores(*items[0])
        outs = []
        for n, (b, h) in enumerate(items):
            following = scores(*items[n + 1]) if n + 1 < len(items) else None
            top = jnp.max(s, axis=1, keepdims=True)
            if b == 1:
                before = tops[yy, h]
                top = jnp.maximum(top, before)
                shrink = jnp.broadcast_to(jnp.exp2((before - top) * EXP_SCALE), (256, 128)).T[0:1]
            p = jnp.exp2((s - top) * EXP_SCALE).astype(BF16)
            if b == 1:
                ot = nt(v_s[h, :, 1024:], p) + part_out[yy, h] * shrink
            else:
                ot = nt(v_s[h], p)
            outs.append(ot[:HD] * (1.0 / ot[HD:HD + 1]))
            if h == 3:
                block = jnp.concatenate(outs, axis=0).astype(BF16)
                outs = []
                for cc in range(2):
                    mas[blocks[b] * 2 + cc] = block[:, cc * 128:(cc + 1) * 128]
                for cc in range(2):
                    send_mixed(blocks[b] * 2 + cc)
            s = following

    own_m = pltpu.make_async_copy(mas.at[ri], my_slot, s_mx.at[ri])
    own_m.start()
    own_m.wait()

    loads["wpa"].wait()

    def project(frames):
        for n, f in enumerate(frames):
            for mm in range(4):
                r = (2 * (f // 2) + mm // 2) * 4 + (f % 2) * 2 + mm % 2

                @pl.when(r != ri)
                def _():
                    slot = mx.at[f, mm * 288:(mm + 1) * 288, :]
                    remote(slot, slot, s_mx.at[r], r_mx.at[f * 4 + mm], (fi, r)).wait_recv()
            ma_n[n * 128:(n + 1) * 128, :] = mx[f].T
        proj = nn(ma_n[:len(frames) * 128, :], wpa_v[...])
        for n, f in enumerate(frames):
            delta = moda[2:3, :] * proj[n * 128:(n + 1) * 128]
            ra[f] = (ta_v[f].astype(F32) + delta).astype(BF16)

    order = [(ri // 4 + 4 - n) % 4 for n in range(4)]
    project(order[:3])
    project(order[3:])

    for k in range(1, 8):
        g = (fi + k) % 8
        at_g = pl.ds(pl.multiple_of(16 * g, 16), 16)
        remote(rbs.at[g], rb.at[:, at_g, :], s_br.at[0], r_br.at[g], (g, ri)).wait_recv()
    for cp in sends:
        cp.wait_send()
    for k in range(1, 16):
        r = (ri + k) % 16
        remote(mas.at[r], mas.at[r], s_mx.at[r], r_mx.at[0], (fi, r)).wait_send()
    own_b.wait()


def per_device(*args):
    any_spec = pl.BlockSpec(memory_space=pl.ANY)
    vmem = pl.BlockSpec(memory_space=pltpu.VMEM)
    v = pltpu.VMEM
    dma = pltpu.SemaphoreType.DMA
    specs = [any_spec, vmem, any_spec, any_spec, vmem]
    return pl.pallas_call(
        kernel,
        out_shape=(v((4, 128, D), BF16), v((4, 128, D), BF16)),
        in_specs=specs + specs,
        out_specs=(vmem, vmem),
        scratch_shapes=[
            v((4, 128, D), BF16),
            v((4, 128, D), BF16),
            v((3, 128, D), BF16),
            v((16, 128, D), BF16),
            v((3, D, 384), BF16),
            v((384, D), BF16),
            v((864, D), BF16),
            v((3, D, 384), BF16),
            v((3 * D, D), BF16),
            v((D, D), BF16),
            v((D, D), BF16),
            v((4, 2048, HD), BF16),
            v((4, HD, 2048), BF16),
            v((4, 80, 2048), BF16),
            v((4, 4, 80, 256), F32),
            v((4, 4, 256, 1), F32),
            v((8, 4, 16, D), BF16),
            v((2, 256, D), BF16),
            v((HEADS, 512, HD), BF16),
            v((HEADS, HD, 512), BF16),
            v((HEADS, 80, 512), BF16),
            v((D, 512), BF16),
            v((8, 4, 16, D), BF16),
            v((16, 288, 128), BF16),
            v((4, D, 128), BF16),
            v((512, D), BF16),
            dma((8,)),
            dma((3,)),
            dma((8,)),
            dma((8,)),
            dma((4,)),
            dma((4, 2)),
            dma((8, 2)),
            dma((16, 2)),
            dma((8,)),
            dma((8,)),
            dma((16,)),
            dma((16,)),
        ],
        compiler_params=pltpu.CompilerParams(
            collective_id=0, has_side_effects=True, vmem_limit_bytes=60 << 20
        ),
        cost_estimate=pl.CostEstimate(
            flops=25_000_000_000, bytes_accessed=40_000_000, transcendentals=20_000_000
        ),
    )(*args)


def solution(mesh):
    tokens = P("frame", "row", None)
    return jax.shard_map(
        per_device,
        mesh=mesh,
        in_specs=(tokens, P(), P(), P(), P(), tokens, P(), P(), P(), P()),
        out_specs=(tokens, tokens),
        check_vma=False,
    )
```
